256 devices in a mesh: dom: 128 (over z, y, x), sub: 2 (over core).
Axes of the slice: x: 4, y: 4, z: 8, core: 2. Of those that a mesh axis runs over, the one named last changes fastest.
Arguments:
- pt_old: float32 [26624, 6, 128], P(('dom', 'sub')), may hold values from -6 to 6
- agg_index: int32 [26624], P(('dom', 'sub')), may hold values from 0 to 16383, as said below
- counts: int32 [256], P(('dom', 'sub')), may hold values from 24 to 104
- tiles_a: bfloat16 [16384, 4, 128, 128], P(('dom', 'sub')), may hold values from -0.5 to 0.5
- tile_cols: int32 [16384, 4], P(('dom', 'sub')), may hold values from 0 to 16383, as said below
- inv_diag: float32 [16384, 128], P(('dom', 'sub')), may hold values from 0.25 to 1
Outputs:
- smoothed: float32 [16384, 4, 6, 128], P(('dom', 'sub'))
The draws below stay inside these ranges and needn't reach their ends.
Inputs may be any that keep to these rules, and one draw needn't show every extreme that they name: `agg_index`: the live slots of all devices name every tile row once. Slots at or beyond the count hold arbitrary numbers. At most 2 live slots of one device name tile rows of one partition (tile row t belongs to partition t // 128). `tile_cols`: slot 0 of tile row t is t itself; every other tile column lies within 16 of t.
All inputs are finite; a program needn't handle non-finite values.
Results may differ from the reference program's by a relative error of at most 0.0018.
Values may be sent and summed in bfloat16 or wider, within the bound.
No kernel may reach another device: no remote copies, remote signals or barrier semaphores. Data moves between devices by JAX's collectives and lax.ppermute only.
A program may use at most 64 MiB of HBM per device.

```python
import math
import jax
import jax.numpy as jnp
from jax import lax

TILE = 128
MODES = 6
NEIGH = 4
TILE_ROWS = 64
PART_ROWS = 128
NTILES = 16384
SLOTS = 104
HALO = 16
N_DOM = 128
N_SUB = 2
DEVICES = 256


def layout(key):
    n_old = N_DOM * N_SUB
    pairs = n_old // 2
    k_delta, k_pick, k_sign, k_perm, k_first = jax.random.split(key, 5)
    spread = TILE_ROWS * 5 // 8
    delta = jax.random.randint(k_delta, (pairs,), 0, spread + 1)
    pick = jax.random.randint(k_pick, (), 0, pairs)
    delta = jnp.where(jnp.arange(pairs) == pick, spread, delta)
    sign = jax.random.randint(k_sign, (pairs,), 0, 2) * 2 - 1
    counts = jnp.concatenate([TILE_ROWS - sign * delta, TILE_ROWS + sign * delta]).astype(jnp.int32)
    starts = jnp.cumsum(counts) - counts
    first = jax.random.randint(k_first, (), 0, N_DOM).astype(jnp.int32)

    def step(last, sub_key):
        order = jax.random.permutation(sub_key, N_DOM).astype(jnp.int32)
        spot = jnp.argmax(order == last)
        order = order.at[spot].set(order[0]).at[0].set(last)
        return (order[N_DOM - 1], order)
    _, rounds = lax.scan(step, first, jax.random.split(k_perm, PART_ROWS))
    slot_ids = jnp.arange(SLOTS, dtype=jnp.int32)
    live = slot_ids[None, :] < counts[:, None]
    spots = jnp.where(live, starts[:, None] + slot_ids[None, :], 0)
    turn = spots // N_DOM
    column = spots % N_DOM
    owner = rounds[turn, column]
    tiles = owner * PART_ROWS + turn
    return (counts, tiles.astype(jnp.int32), live)


def draw_agg_index(key, part):
    counts, tiles, live = layout(key)
    key = jax.random.fold_in(key, 7)
    junk = jax.random.randint(key, tiles.shape, 0, NTILES).astype(jnp.int32)
    return jnp.where(live, tiles, junk).reshape(-1).astype(jnp.int32)


def draw_counts(key, part):
    counts, tiles, live = layout(key)
    return counts.astype(jnp.int32)


def draw_tile_cols(key, part):
    key = jax.random.fold_in(key, 5)
    k_off, k_sign = jax.random.split(key, 2)
    rows = jnp.arange(NTILES, dtype=jnp.int32)[:, None]
    offset = jax.random.randint(k_off, (NTILES, NEIGH - 1), 1, HALO + 1).astype(jnp.int32)
    sign = (jax.random.randint(k_sign, (NTILES, NEIGH - 1), 0, 2) * 2 - 1).astype(jnp.int32)
    others = rows + sign * offset
    others = jnp.where((others < 0) | (others >= NTILES), rows - sign * offset, others)
    return jnp.concatenate([rows, others], axis=1).astype(jnp.int32)


def level_of(rng, shape, cuts, smallest, high):
    factor_of = 1.0
    for axis_at, blocks in cuts:
        steps = jax.random.uniform(jax.random.fold_in(jax.random.fold_in(rng, 6), axis_at), (blocks,), jnp.float32, smallest / len(cuts), high / len(cuts))
        factor_of = factor_of * jnp.repeat(jnp.exp(steps), shape[axis_at] // blocks).reshape((-1,) + (1,) * (len(shape) - 1 - axis_at))
    return factor_of


def gaussian(stream_key, shape, scale, reach, cuts=(), kind=jnp.bfloat16):
    loudness = level_of(stream_key, shape, cuts, -0.22, 0.18) if cuts else 1.0
    array = jax.random.normal(stream_key, shape, jnp.float32) * scale * loudness
    return jnp.minimum(jnp.maximum(array, -reach), reach).astype(kind)


def setup_inputs(seed: int = 0) -> dict:
    seeds = jax.random.split(jax.random.key(seed), 7)
    pt_old = gaussian(seeds[0], (DEVICES * SLOTS, MODES, TILE), 1.0, 6.0, ((0, 256),), jnp.float32)
    agg_index = draw_agg_index(jax.random.fold_in(seeds[6], 71), 0)
    counts = draw_counts(jax.random.fold_in(seeds[6], 71), 0)
    tiles_a = gaussian(seeds[3], (NTILES, NEIGH, TILE, TILE), TILE ** -0.5, 0.5, ((0, 256),))
    tile_cols = draw_tile_cols(jax.random.fold_in(seeds[6], 71), 0)
    inv_diag = jnp.clip(jnp.exp(math.log(1.0) - 1.3862944 * jax.random.uniform(seeds[5], (NTILES, TILE), jnp.float32) ** level_of(seeds[5], (NTILES, TILE), ((0, 256),), -0.2, 0.2)), 0.25, 1.0)
    return dict(pt_old=pt_old, agg_index=agg_index, counts=counts, tiles_a=tiles_a, tile_cols=tile_cols, inv_diag=inv_diag)


DAMPING = 2.0 / 3.0


def reference(pt_old, agg_index, counts, tiles_a, tile_cols, inv_diag):
    n_old = counts.shape[0]
    total = pt_old.shape[0]
    slot_ids = jnp.arange(total, dtype=jnp.int32) % SLOTS
    holder = jnp.arange(total, dtype=jnp.int32) // SLOTS
    live = slot_ids < counts[holder]
    target = jnp.where(live, agg_index, NTILES).astype(jnp.int32)
    placed = jnp.zeros((NTILES + 1, MODES, TILE), jnp.float32).at[target].set(pt_old)[:NTILES]
    rounded = placed.astype(jnp.bfloat16)

    def block(start):
        tiles = lax.dynamic_slice_in_dim(tiles_a, start, TILE_ROWS, 0).astype(jnp.float32)
        columns = lax.dynamic_slice_in_dim(tile_cols, start, TILE_ROWS, 0)
        scales = lax.dynamic_slice_in_dim(inv_diag, start, TILE_ROWS, 0)
        own = lax.dynamic_slice_in_dim(placed, start, TILE_ROWS, 0)
        gathered = rounded[columns].astype(jnp.float32)
        product = jnp.einsum("tkcj,tkij->tkci", gathered, tiles, precision=lax.Precision.HIGHEST)
        smooth = -DAMPING * scales[:, None, None, :] * product
        return smooth.at[:, 0].add(own)

    starts = jnp.arange(NTILES // TILE_ROWS, dtype=jnp.int32) * TILE_ROWS
    blocks = lax.map(block, starts)
    return blocks.reshape(NTILES, NEIGH, MODES, TILE)
```

```python
import jax
import jax.numpy as jnp
from jax import lax
from jax.experimental import pallas as pl
from jax.experimental.pallas import tpu as pltpu
from jax.sharding import PartitionSpec as P

DAMPING = 2.0 / 3.0
BF16 = jnp.bfloat16
F32 = jnp.float32
VMEM = pltpu.VMEM
SMEM = pltpu.SMEM

LANES = 128
MSG_ROWS = 16


def iota(shape, dim):
    return lax.broadcasted_iota(jnp.int32, shape, dim)


def dot(a, b, dims):
    return lax.dot_general(a, b, (dims, ((), ())), preferred_element_type=F32)


def onehot(cond):
    return jnp.where(cond, 1.0, 0.0).astype(BF16)


def pack_kernel(count_ref, agg_ref, pt_ref, out_ref, wide):
    modes, slots, _ = pt_ref.shape
    n_dom = out_ref.shape[0]
    agg = agg_ref[...]
    live = iota((1, slots), 1) < count_ref[0]
    owner = jnp.where(live, agg // LANES, -1)
    position = agg % LANES
    to_dest = owner == iota((n_dom, slots), 0)
    before = onehot(iota((slots, slots), 0) < iota((slots, slots), 1))
    rank = dot(onehot(to_dest), before, ((1,), (0,)))
    first = onehot(to_dest & (rank < 0.5))
    second = onehot(to_dest & (rank > 0.5))
    pick = jnp.concatenate([first, second], axis=0)
    at = onehot(position == iota((LANES, slots), 0))
    where_to = dot(pick, at, ((1,), (1,)))
    blocks = jnp.concatenate([pt_ref[c].astype(BF16) for c in range(modes)], axis=1)
    sent = dot(pick, blocks, ((1,), (0,)))
    for r in range(2):
        rows = slice(r * n_dom, (r + 1) * n_dom)
        for c in range(modes):
            wide[pl.ds(r * modes + c, n_dom, stride=MSG_ROWS), :] = sent[rows, c * LANES : (c + 1) * LANES]
        wide[pl.ds(2 * modes + r, n_dom, stride=MSG_ROWS), :] = where_to[rows]
    for r in range(2 * modes + 2, MSG_ROWS):
        wide[pl.ds(r, n_dom, stride=MSG_ROWS), :] = jnp.zeros((n_dom, LANES), F32)
    out_ref[...] = wide[...].reshape(out_ref.shape).astype(BF16)


def place_kernel(sub_ref, msg_ref, mine_ref, peer_ref, edge_a_ref, edge_b_ref, wide, placed):
    n_dom = msg_ref.shape[0]
    modes = (MSG_ROWS - 2) // 2 - 1
    keep, halo = mine_ref.shape[0], edge_a_ref.shape[0]
    part = LANES
    sub = sub_ref[0]
    wide[...] = msg_ref[...].astype(F32).reshape(wide.shape)

    def column(row):
        return wide[pl.ds(row, n_dom, stride=MSG_ROWS), :].astype(BF16)

    at = jnp.concatenate([column(2 * modes + r) for r in range(2)], axis=0)
    blocks = jnp.concatenate(
        [jnp.concatenate([column(r * modes + c) for c in range(modes)], axis=1) for r in range(2)], axis=0
    )
    placed[...] = dot(at, blocks, ((0,), (0,)))
    low = pl.multiple_of(sub * (part - keep), 16)
    mine_ref[...] = placed[pl.ds(low, keep), :].astype(BF16)
    other = pl.multiple_of((1 - sub) * (part - keep), 16)
    peer_ref[...] = placed[pl.ds(other, keep), :].astype(BF16)
    far = pl.multiple_of((1 - sub) * (part - halo), 16)
    near = pl.multiple_of(sub * (part - halo), 16)
    edge_a_ref[...] = placed[pl.ds(far, halo), :].astype(BF16)
    edge_b_ref[...] = placed[pl.ds(near, halo), :].astype(BF16)


def smooth_kernel(base_ref, cols_ref, mine_ref, peer_ref, edge_a_ref, edge_b_ref, diag_ref, tiles_ref, out_ref, left):
    step = pl.program_id(0)
    n_tile, rows, _ = out_ref.shape
    neigh = tiles_ref.shape[1]
    modes = rows // neigh
    total = cols_ref.shape[1]
    keep, halo = mine_ref.shape[0], edge_a_ref.shape[0]
    n_ext = keep + halo

    @pl.when(step == 0)
    def _():
        ext = jnp.concatenate(
            [mine_ref[...] + peer_ref[...], edge_a_ref[...] + edge_b_ref[...]], axis=0
        )
        local = cols_ref[...] - base_ref[0]
        local = jnp.where(local < 0, local + n_ext, local)
        for k in range(neigh):
            take = onehot(iota((n_ext, total), 0) == local[k : k + 1, :])
            got = dot(take, ext, ((0,), (0,)))
            for c in range(modes):
                left[pl.ds(c * neigh + k, total, stride=rows), :] = got[:, c * LANES : (c + 1) * LANES]

    row_k = iota((rows, LANES), 0) % neigh
    for n in range(n_tile):
        t = step * n_tile + n
        lhs = left[pl.ds(pl.multiple_of(t * rows, 8), rows), :]
        tiles = tiles_ref[n].reshape(neigh * LANES, LANES)
        every = dot(lhs.astype(BF16), tiles, ((1,), (1,)))
        product = every[:, :LANES]
        for k in range(1, neigh):
            product = jnp.where(row_k == k, every[:, k * LANES : (k + 1) * LANES], product)
        scale = -DAMPING * diag_ref[pl.ds(n, 1), :]
        out_ref[n] = scale * product + jnp.where(row_k == 0, lhs, 0.0)


def per_device(pt_old, agg_index, counts, tiles_a, tile_cols, inv_diag):
    n_dom = lax.axis_size("dom")
    n_sub = lax.axis_size("sub")
    slots, modes, width = pt_old.shape
    rows_dev, neigh = tile_cols.shape
    halo = rows_dev // 4
    keep = rows_dev + halo
    sub = lax.axis_index("sub")
    device = lax.axis_index("dom") * n_sub + sub
    vmem = pl.BlockSpec(memory_space=VMEM)
    smem = pl.BlockSpec(memory_space=SMEM)

    messages = pl.pallas_call(
        pack_kernel,
        out_shape=jax.ShapeDtypeStruct((n_dom, MSG_ROWS, width), BF16),
        in_specs=[smem, vmem, vmem],
        out_specs=vmem,
        scratch_shapes=[VMEM((n_dom * MSG_ROWS, width), F32)],
        name="pack",
    )(counts, agg_index.reshape(1, slots), jnp.transpose(pt_old, (1, 0, 2)))

    arrived = lax.all_to_all(messages, "dom", split_axis=0, concat_axis=0, tiled=True)

    flat = modes * width
    mine, for_peer, edge_a, edge_b = pl.pallas_call(
        place_kernel,
        out_shape=[jax.ShapeDtypeStruct((n, flat), BF16) for n in (keep, keep, halo, halo)],
        in_specs=[smem, vmem],
        out_specs=[vmem] * 4,
        scratch_shapes=[VMEM((n_dom * MSG_ROWS, width), F32), VMEM((LANES, flat), F32)],
        name="place",
    )(sub.reshape(1), arrived)

    n_dev = n_dom * n_sub
    both = ("dom", "sub")
    peer = lax.ppermute(for_peer, both, [(i, i ^ 1) for i in range(n_dev)])
    same, cross = [], []
    for p in range(n_dom):
        if p + 1 < n_dom:
            same.append((2 * p, 2 * p + 2))
            cross.append((2 * p + 1, 2 * p + 2))
        if p > 0:
            same.append((2 * p + 1, 2 * p - 1))
            cross.append((2 * p, 2 * p - 1))
    edge_a = lax.ppermute(edge_a, both, same)
    edge_b = lax.ppermute(edge_b, both, cross)

    base = device * rows_dev - sub * halo
    per_step = 8
    whole = lambda shape: pl.BlockSpec(shape, lambda i: (0,) * len(shape))
    out = pl.pallas_call(
        smooth_kernel,
        out_shape=jax.ShapeDtypeStruct((rows_dev, modes * neigh, width), F32),
        grid=(rows_dev // per_step,),
        in_specs=[
            smem,
            whole((neigh, rows_dev)),
            whole((keep, flat)),
            whole((keep, flat)),
            whole((halo, flat)),
            whole((halo, flat)),
            pl.BlockSpec((per_step, width), lambda i: (i, 0)),
            pl.BlockSpec((per_step, neigh, width, width), lambda i: (i, 0, 0, 0)),
        ],
        out_specs=pl.BlockSpec((per_step, modes * neigh, width), lambda i: (i, 0, 0)),
        scratch_shapes=[VMEM((rows_dev * modes * neigh, width), F32)],
        name="smooth",
    )(base.reshape(1), tile_cols.T, mine, peer, edge_a, edge_b, inv_diag, tiles_a)
    return jnp.transpose(out.reshape(rows_dev, modes, neigh, width), (0, 2, 1, 3))


def solution(mesh):
    in_specs = (
        P(("dom", "sub"), None, None),
        P(("dom", "sub")),
        P(("dom", "sub")),
        P(("dom", "sub"), None, None, None),
        P(("dom", "sub"), None),
        P(("dom", "sub"), None),
    )
    out_specs = P(("dom", "sub"), None, None, None)
    return jax.shard_map(
        per_device, mesh=mesh, in_specs=in_specs, out_specs=out_specs, check_vma=False
    )
```

```python
import jax
import jax.numpy as jnp
from jax import lax
from jax.experimental import pallas as pl
from jax.experimental.pallas import tpu as pltpu
from jax.sharding import PartitionSpec as P

DAMPING = 2.0 / 3.0
BF16 = jnp.bfloat16
F32 = jnp.float32
VMEM = pltpu.VMEM
SMEM = pltpu.SMEM

LANES = 128
MIB = 2**20
PARAMS = pltpu.CompilerParams(vmem_limit_bytes=20 * MIB)
WIDE = pltpu.CompilerParams(vmem_limit_bytes=60 * MIB)
MSG_ROWS = 14


def iota(shape, dim):
    return lax.broadcasted_iota(jnp.int32, shape, dim)


def dot(a, b, dims):
    return lax.dot_general(a, b, (dims, ((), ())), preferred_element_type=F32)


def onehot(cond):
    return jnp.where(cond, 1.0, 0.0).astype(BF16)


def pack_kernel(count_hbm, agg_hbm, pt_hbm, out_ref, wide, count_ref, agg_ref, pt_ref, sems):
    modes, slots, _ = pt_ref.shape
    n_dom = out_ref.shape[0] // MSG_ROWS
    copies = [
        pltpu.make_async_copy(count_hbm, count_ref, sems.at[0]),
        pltpu.make_async_copy(agg_hbm, agg_ref, sems.at[1]),
        pltpu.make_async_copy(pt_hbm, pt_ref, sems.at[2]),
    ]
    for copy in copies:
        copy.start()
    copies[0].wait()
    copies[1].wait()
    agg = agg_ref[...]
    live = iota((1, slots), 1) < count_ref[0]
    owner = jnp.where(live, agg // LANES, -1)
    position = agg % LANES
    to_dest = owner == iota((n_dom, slots), 0)
    before = onehot(iota((slots, slots), 0) < iota((slots, slots), 1))
    rank = dot(onehot(to_dest), before, ((1,), (0,)))
    first = onehot(to_dest & (rank < 0.5))
    second = onehot(to_dest & (rank > 0.5))
    pick = jnp.concatenate([first, second], axis=0)
    at = onehot(position == iota((LANES, slots), 0))
    where_to = dot(pick, at, ((1,), (1,)))
    copies[2].wait()
    blocks = jnp.concatenate([pt_ref[c].astype(BF16) for c in range(modes)], axis=1)
    sent = dot(pick, blocks, ((1,), (0,)))
    for r in range(2):
        rows = slice(r * n_dom, (r + 1) * n_dom)
        for c in range(modes):
            wide[pl.ds(r * modes + c, n_dom, stride=MSG_ROWS), :] = sent[rows, c * LANES : (c + 1) * LANES]
        wide[pl.ds(2 * modes + r, n_dom, stride=MSG_ROWS), :] = where_to[rows]
    out_ref[...] = wide[...].astype(BF16)


def place_kernel(sub_ref, msg_ref, mine_ref, peer_ref, wide, placed):
    n_dom = msg_ref.shape[0] // MSG_ROWS
    modes = MSG_ROWS // 2 - 1
    keep = mine_ref.shape[0]
    sub = sub_ref[0]
    wide[...] = msg_ref[...].astype(F32)

    def column(row):
        return wide[pl.ds(row, n_dom, stride=MSG_ROWS), :].astype(BF16)

    at = jnp.concatenate([column(2 * modes + r) for r in range(2)], axis=0)
    blocks = jnp.concatenate(
        [jnp.concatenate([column(r * modes + c) for c in range(modes)], axis=1) for r in range(2)], axis=0
    )
    placed[...] = dot(at, blocks, ((0,), (0,)))
    low = pl.multiple_of(sub * (LANES - keep), 16)
    mine_ref[...] = placed[pl.ds(low, keep), :].astype(BF16)
    other = pl.multiple_of((1 - sub) * (LANES - keep), 16)
    peer_ref[...] = placed[pl.ds(other, keep), :].astype(BF16)


def edge_kernel(sub_ref, mine_ref, peer_ref, edge_ref):
    keep, halo = mine_ref.shape[0], edge_ref.shape[0]
    low = pl.multiple_of(sub_ref[0] * (keep - halo), 16)
    edge_ref[...] = mine_ref[pl.ds(low, halo), :] + peer_ref[pl.ds(low, halo), :]


def turn_kernel(tiles_ref, out_ref):
    n_tile, neigh, width, _ = tiles_ref.shape
    for n in range(n_tile):
        for k in range(neigh):
            out_ref[n, k * width : (k + 1) * width, :] = tiles_ref[n, k].T


def gather(ext, local, left, neigh, modes):
    total = local.shape[1]
    for k in range(neigh):
        take = onehot(iota((ext.shape[0], total), 0) == local[k : k + 1, :])
        got = dot(take, ext, ((0,), (0,)))
        for c in range(modes):
            left[pl.ds(c * neigh + k, total, stride=modes * neigh), :] = got[:, c * LANES : (c + 1) * LANES]


def smooth_row(t, left, tiles, diag_ref, neigh, rows):
    lhs = left[pl.ds(pl.multiple_of(t * rows, 8), rows), :]
    row_k = iota((rows, LANES), 0) % neigh
    spread = jnp.concatenate([jnp.where(row_k == k, lhs, 0.0).astype(BF16) for k in range(neigh)], axis=1)
    product = dot(spread, tiles, ((1,), (0,)))
    scale = -DAMPING * diag_ref[pl.ds(t, 1), :]
    return scale * product + jnp.where(row_k == 0, lhs, 0.0)


def inner_kernel(
    sub_ref, base_ref, cols_ref, mine_ref, peer_ref, diag_ref, tiles_hbm, out_hbm, rest_ref, left, tiles, done, in_sems, out_sems
):
    count, rows, _ = done.shape
    neigh, total = cols_ref.shape
    rest = total - count
    modes = rows // neigh
    chunk = count // (in_sems.shape[0] - 1)
    sub = sub_ref[0]
    start = (1 - sub) * rest

    fetches = []
    for i in range(count // chunk):
        place = pl.ds(i * chunk, chunk)
        fetches.append(pltpu.make_async_copy(tiles_hbm.at[pl.ds(start + i * chunk, chunk)], tiles.at[place], in_sems.at[i]))
    fetches.append(pltpu.make_async_copy(tiles_hbm.at[pl.ds(sub * count, rest)], rest_ref, in_sems.at[count // chunk]))
    for fetch in fetches:
        fetch.start()

    gather(mine_ref[...] + peer_ref[...], cols_ref[...] - base_ref[0], left, neigh, modes)

    writes = []
    for i in range(count // chunk):
        fetches[i].wait()
        for n in range(i * chunk, (i + 1) * chunk):
            done[n] = smooth_row(start + n, left, tiles[n], diag_ref, neigh, rows)
        place = pl.ds(i * chunk, chunk)
        writes.append(pltpu.make_async_copy(done.at[place], out_hbm.at[pl.ds(start + i * chunk, chunk)], out_sems.at[i]))
        writes[-1].start()
    fetches[-1].wait()
    for write in writes:
        write.wait()


def outer_kernel(
    sub_ref, base_ref, cols_ref, mine_ref, peer_ref, edge_ref, diag_ref, rest_ref, begun_hbm, out_hbm, left, done, sem
):
    del begun_hbm
    rest, rows, _ = done.shape
    neigh, total = cols_ref.shape
    modes = rows // neigh
    start = sub_ref[0] * (total - rest)
    ext = jnp.concatenate([mine_ref[...] + peer_ref[...], edge_ref[...]], axis=0)
    local = cols_ref[...] - base_ref[0]
    gather(ext, jnp.where(local < 0, local + ext.shape[0], local), left, neigh, modes)
    for n in range(rest):
        done[n] = smooth_row(start + n, left, rest_ref[n], diag_ref, neigh, rows)
    write = pltpu.make_async_copy(done, out_hbm.at[pl.ds(start, rest)], sem)
    write.start()
    write.wait()


def per_device(pt_old, agg_index, counts, tiles_a, tile_cols, inv_diag):
    n_dom = lax.axis_size("dom")
    n_sub = lax.axis_size("sub")
    slots, modes, width = pt_old.shape
    rows_dev, neigh = tile_cols.shape
    halo = rows_dev // 4
    keep = rows_dev + halo
    sub = lax.axis_index("sub")
    device = lax.axis_index("dom") * n_sub + sub
    vmem = pl.BlockSpec(memory_space=VMEM)
    smem = pl.BlockSpec(memory_space=SMEM)

    hbm = pl.BlockSpec(memory_space=pl.ANY)
    flat = modes * width
    msg_shape = (n_dom * MSG_ROWS, width)
    messages = pl.pallas_call(
        pack_kernel,
        out_shape=jax.ShapeDtypeStruct(msg_shape, BF16),
        in_specs=[hbm, hbm, hbm],
        out_specs=vmem,
        scratch_shapes=[
            VMEM(msg_shape, F32),
            SMEM((1,), jnp.int32),
            VMEM((1, slots), jnp.int32),
            VMEM((modes, slots, width), F32),
            pltpu.SemaphoreType.DMA((3,)),
        ],
        compiler_params=WIDE,
        name="pack",
    )(counts, agg_index.reshape(1, slots), jnp.transpose(pt_old, (1, 0, 2)))

    messages, tiles_a = lax.optimization_barrier((messages, tiles_a))
    arrived = lax.all_to_all(
        messages.reshape(n_dom, MSG_ROWS // 2, 2, width), "dom", split_axis=0, concat_axis=0, tiled=True
    ).reshape(msg_shape)

    per_step = 16
    turned = pl.pallas_call(
        turn_kernel,
        out_shape=jax.ShapeDtypeStruct((rows_dev, neigh * width, width), BF16),
        grid=(rows_dev // per_step,),
        in_specs=[pl.BlockSpec((per_step, neigh, width, width), lambda i: (i, 0, 0, 0))],
        out_specs=pl.BlockSpec((per_step, neigh * width, width), lambda i: (i, 0, 0)),
        compiler_params=WIDE,
        cost_estimate=pl.CostEstimate(flops=0, bytes_accessed=2 * tiles_a.size * 2, transcendentals=0),
        name="turn",
    )(tiles_a)
    arrived, turned = lax.optimization_barrier((arrived, turned))

    mine, for_peer = pl.pallas_call(
        place_kernel,
        out_shape=[jax.ShapeDtypeStruct((keep, flat), BF16)] * 2,
        in_specs=[smem, vmem],
        out_specs=[vmem] * 2,
        scratch_shapes=[VMEM(msg_shape, F32), VMEM((LANES, flat), F32)],
        compiler_params=PARAMS,
        name="place",
    )(sub.reshape(1), arrived)

    n_dev = n_dom * n_sub
    both = ("dom", "sub")
    peer = lax.ppermute(for_peer, both, [(i, i ^ 1) for i in range(n_dev)])
    edge = pl.pallas_call(
        edge_kernel,
        out_shape=jax.ShapeDtypeStruct((halo, flat), BF16),
        in_specs=[smem, vmem, vmem],
        out_specs=vmem,
        compiler_params=PARAMS,
        name="edge",
    )(sub.reshape(1), mine, peer)
    across = [pair for i in range(1, n_dev - 1, 2) for pair in ((i, i + 1), (i + 1, i))]
    edge = lax.ppermute(edge, both, across)

    base = device * rows_dev - sub * halo
    rows = modes * neigh
    inner = rows_dev - halo
    chunk = 8
    out_shape = jax.ShapeDtypeStruct((rows_dev, rows, width), F32)
    left_shape = VMEM((rows_dev * rows, width), F32)
    begun, rest = pl.pallas_call(
        inner_kernel,
        out_shape=[out_shape, jax.ShapeDtypeStruct((halo, neigh * width, width), BF16)],
        in_specs=[smem, smem] + [vmem] * 4 + [hbm],
        out_specs=[hbm, vmem],
        scratch_shapes=[
            left_shape,
            VMEM((inner, neigh * width, width), BF16),
            VMEM((inner, rows, width), F32),
            pltpu.SemaphoreType.DMA((inner // chunk + 1,)),
            pltpu.SemaphoreType.DMA((inner // chunk,)),
        ],
        compiler_params=pltpu.CompilerParams(vmem_limit_bytes=48 * MIB),
        cost_estimate=pl.CostEstimate(
            flops=2 * inner * rows * neigh * width * width, bytes_accessed=tiles_a.size * 2, transcendentals=0
        ),
        name="inner",
    )(sub.reshape(1), base.reshape(1), tile_cols.T, mine, peer, inv_diag, turned)
    out = pl.pallas_call(
        outer_kernel,
        out_shape=out_shape,
        in_specs=[smem, smem] + [vmem] * 6 + [hbm],
        out_specs=hbm,
        scratch_shapes=[left_shape, VMEM((halo, rows, width), F32), pltpu.SemaphoreType.DMA],
        input_output_aliases={8: 0},
        compiler_params=PARAMS,
        name="outer",
    )(sub.reshape(1), base.reshape(1), tile_cols.T, mine, peer, edge, inv_diag, rest, begun)
    return jnp.transpose(out.reshape(rows_dev, modes, neigh, width), (0, 2, 1, 3))


def solution(mesh):
    in_specs = (
        P(("dom", "sub"), None, None),
        P(("dom", "sub")),
        P(("dom", "sub")),
        P(("dom", "sub"), None, None, None),
        P(("dom", "sub"), None),
        P(("dom", "sub"), None),
    )
    out_specs = P(("dom", "sub"), None, None, None)
    return jax.shard_map(
        per_device, mesh=mesh, in_specs=in_specs, out_specs=out_specs, check_vma=False
    )
```

```python
import jax
import jax.numpy as jnp
from jax import lax
from jax.experimental import pallas as pl
from jax.experimental.pallas import tpu as pltpu
from jax.sharding import PartitionSpec as P

DAMPING = 2.0 / 3.0
BF16 = jnp.bfloat16
F32 = jnp.float32
VMEM = pltpu.VMEM
SMEM = pltpu.SMEM

LANES = 128
MIB = 2**20
PARAMS = pltpu.CompilerParams(vmem_limit_bytes=20 * MIB)
WIDE = pltpu.CompilerParams(vmem_limit_bytes=60 * MIB)
MSG_ROWS = 14


def partition_of(message):
    z, x, y = message % 8, message // 8 % 4, message // 32
    return 127 - (z * 16 + y * 4 + x)


ORDER = [partition_of(i) for i in range(128)]


def iota(shape, dim):
    return lax.broadcasted_iota(jnp.int32, shape, dim)


def dot(a, b, dims):
    return lax.dot_general(a, b, (dims, ((), ())), preferred_element_type=F32)


def onehot(cond):
    return jnp.where(cond, 1.0, 0.0).astype(BF16)


def pack_kernel(count_hbm, agg_hbm, pt_hbm, out_ref, wide, count_ref, agg_ref, pt_ref, sems):
    modes, slots, _ = pt_ref.shape
    n_dom = out_ref.shape[0] // MSG_ROWS
    copies = [
        pltpu.make_async_copy(count_hbm, count_ref, sems.at[0]),
        pltpu.make_async_copy(agg_hbm, agg_ref, sems.at[1]),
        pltpu.make_async_copy(pt_hbm, pt_ref, sems.at[2]),
    ]
    for copy in copies:
        copy.start()
    copies[0].wait()
    copies[1].wait()
    agg = agg_ref[...]
    live = iota((1, slots), 1) < count_ref[0]
    owner = jnp.where(live, agg // LANES, -1)
    position = agg % LANES
    to_dest = owner == partition_of(iota((n_dom, slots), 0))
    before = onehot(iota((slots, slots), 0) < iota((slots, slots), 1))
    rank = dot(onehot(to_dest), before, ((1,), (0,)))
    first = onehot(to_dest & (rank < 0.5))
    second = onehot(to_dest & (rank > 0.5))
    pick = jnp.concatenate([first, second], axis=0)
    at = onehot(position == iota((LANES, slots), 0))
    where_to = dot(pick, at, ((1,), (1,)))
    copies[2].wait()
    blocks = jnp.concatenate([pt_ref[c].astype(BF16) for c in range(modes)], axis=1)
    sent = dot(pick, blocks, ((1,), (0,)))
    for r in range(2):
        rows = slice(r * n_dom, (r + 1) * n_dom)
        for c in range(modes):
            wide[pl.ds(r * modes + c, n_dom, stride=MSG_ROWS), :] = sent[rows, c * LANES : (c + 1) * LANES]
        wide[pl.ds(2 * modes + r, n_dom, stride=MSG_ROWS), :] = where_to[rows]
    out_ref[...] = wide[...].astype(BF16)


def place_kernel(sub_ref, msg_ref, mine_ref, peer_ref, wide, placed):
    n_dom = msg_ref.shape[0] // MSG_ROWS
    modes = MSG_ROWS // 2 - 1
    keep = mine_ref.shape[0]
    sub = sub_ref[0]
    wide[...] = msg_ref[...].astype(F32)

    def column(row):
        return wide[pl.ds(row, n_dom, stride=MSG_ROWS), :].astype(BF16)

    at = jnp.concatenate([column(2 * modes + r) for r in range(2)], axis=0)
    blocks = jnp.concatenate(
        [jnp.concatenate([column(r * modes + c) for c in range(modes)], axis=1) for r in range(2)], axis=0
    )
    placed[...] = dot(at, blocks, ((0,), (0,)))
    low = pl.multiple_of(sub * (LANES - keep), 16)
    mine_ref[...] = placed[pl.ds(low, keep), :].astype(BF16)
    other = pl.multiple_of((1 - sub) * (LANES - keep), 16)
    peer_ref[...] = placed[pl.ds(other, keep), :].astype(BF16)


def edge_kernel(sub_ref, mine_ref, peer_ref, edge_ref):
    keep, halo = mine_ref.shape[0], edge_ref.shape[0]
    low = pl.multiple_of(sub_ref[0] * (keep - halo), 16)
    edge_ref[...] = mine_ref[pl.ds(low, halo), :] + peer_ref[pl.ds(low, halo), :]


def turn_kernel(tiles_ref, out_ref):
    n_tile, neigh, width, _ = tiles_ref.shape
    for n in range(n_tile):
        for k in range(neigh):
            out_ref[n, k * width : (k + 1) * width, :] = tiles_ref[n, k].T


def gather(ext, local, left, neigh, modes):
    total = local.shape[1]
    for k in range(neigh):
        take = onehot(iota((ext.shape[0], total), 0) == local[k : k + 1, :])
        got = dot(take, ext, ((0,), (0,)))
        for c in range(modes):
            left[pl.ds(c * neigh + k, total, stride=modes * neigh), :] = got[:, c * LANES : (c + 1) * LANES]


def smooth_row(t, left, tiles, diag_ref, neigh, rows):
    lhs = left[pl.ds(pl.multiple_of(t * rows, 8), rows), :]
    row_k = iota((rows, LANES), 0) % neigh
    spread = jnp.concatenate([jnp.where(row_k == k, lhs, 0.0).astype(BF16) for k in range(neigh)], axis=1)
    product = dot(spread, tiles, ((1,), (0,)))
    scale = -DAMPING * diag_ref[pl.ds(t, 1), :]
    return scale * product + jnp.where(row_k == 0, lhs, 0.0)


def inner_kernel(
    sub_ref, base_ref, cols_ref, mine_ref, peer_ref, diag_ref, tiles_hbm, out_hbm, rest_ref, left, tiles, done, in_sems, out_sems
):
    count, rows, _ = done.shape
    neigh, total = cols_ref.shape
    rest = total - count
    modes = rows // neigh
    chunk = count // (in_sems.shape[0] - 1)
    sub = sub_ref[0]
    start = (1 - sub) * rest

    fetches = []
    for i in range(count // chunk):
        place = pl.ds(i * chunk, chunk)
        fetches.append(pltpu.make_async_copy(tiles_hbm.at[pl.ds(start + i * chunk, chunk)], tiles.at[place], in_sems.at[i]))
    fetches.append(pltpu.make_async_copy(tiles_hbm.at[pl.ds(sub * count, rest)], rest_ref, in_sems.at[count // chunk]))
    for fetch in fetches:
        fetch.start()

    gather(mine_ref[...] + peer_ref[...], cols_ref[...] - base_ref[0], left, neigh, modes)

    writes = []
    for i in range(count // chunk):
        fetches[i].wait()
        for n in range(i * chunk, (i + 1) * chunk):
            done[n] = smooth_row(start + n, left, tiles[n], diag_ref, neigh, rows)
        place = pl.ds(i * chunk, chunk)
        writes.append(pltpu.make_async_copy(done.at[place], out_hbm.at[pl.ds(start + i * chunk, chunk)], out_sems.at[i]))
        writes[-1].start()
    fetches[-1].wait()
    for write in writes:
        write.wait()


def outer_kernel(
    sub_ref, base_ref, cols_ref, mine_ref, peer_ref, edge_ref, diag_ref, rest_ref, begun_hbm, out_hbm, left, done, sem
):
    del begun_hbm
    rest, rows, _ = done.shape
    neigh, total = cols_ref.shape
    modes = rows // neigh
    start = sub_ref[0] * (total - rest)
    ext = jnp.concatenate([mine_ref[...] + peer_ref[...], edge_ref[...]], axis=0)
    local = cols_ref[...] - base_ref[0]
    gather(ext, jnp.where(local < 0, local + ext.shape[0], local), left, neigh, modes)
    for n in range(rest):
        done[n] = smooth_row(start + n, left, rest_ref[n], diag_ref, neigh, rows)
    write = pltpu.make_async_copy(done, out_hbm.at[pl.ds(start, rest)], sem)
    write.start()
    write.wait()


def per_device(pt_old, agg_index, counts, tiles_a, tile_cols, inv_diag):
    n_dom = lax.axis_size("dom")
    n_sub = lax.axis_size("sub")
    slots, modes, width = pt_old.shape
    rows_dev, neigh = tile_cols.shape
    halo = rows_dev // 4
    keep = rows_dev + halo
    sub = lax.axis_index("sub")
    device = lax.axis_index("dom") * n_sub + sub
    vmem = pl.BlockSpec(memory_space=VMEM)
    smem = pl.BlockSpec(memory_space=SMEM)

    hbm = pl.BlockSpec(memory_space=pl.ANY)
    flat = modes * width
    msg_shape = (n_dom * MSG_ROWS, width)
    messages = pl.pallas_call(
        pack_kernel,
        out_shape=jax.ShapeDtypeStruct(msg_shape, BF16),
        in_specs=[hbm, hbm, hbm],
        out_specs=vmem,
        scratch_shapes=[
            VMEM(msg_shape, F32),
            SMEM((1,), jnp.int32),
            VMEM((1, slots), jnp.int32),
            VMEM((modes, slots, width), F32),
            pltpu.SemaphoreType.DMA((3,)),
        ],
        compiler_params=WIDE,
        name="pack",
    )(counts, agg_index.reshape(1, slots), jnp.transpose(pt_old, (1, 0, 2)))

    messages, tiles_a = lax.optimization_barrier((messages, tiles_a))
    arrived = lax.all_to_all(
        messages.reshape(n_dom, MSG_ROWS // 2, 2, width),
        "dom",
        split_axis=0,
        concat_axis=0,
        tiled=True,
        axis_index_groups=[ORDER],
    ).reshape(msg_shape)

    per_step = 16
    turned = pl.pallas_call(
        turn_kernel,
        out_shape=jax.ShapeDtypeStruct((rows_dev, neigh * width, width), BF16),
        grid=(rows_dev // per_step,),
        in_specs=[pl.BlockSpec((per_step, neigh, width, width), lambda i: (i, 0, 0, 0))],
        out_specs=pl.BlockSpec((per_step, neigh * width, width), lambda i: (i, 0, 0)),
        compiler_params=WIDE,
        cost_estimate=pl.CostEstimate(flops=0, bytes_accessed=2 * tiles_a.size * 2, transcendentals=0),
        name="turn",
    )(tiles_a)
    arrived, turned = lax.optimization_barrier((arrived, turned))

    mine, for_peer = pl.pallas_call(
        place_kernel,
        out_shape=[jax.ShapeDtypeStruct((keep, flat), BF16)] * 2,
        in_specs=[smem, vmem],
        out_specs=[vmem] * 2,
        scratch_shapes=[VMEM(msg_shape, F32), VMEM((LANES, flat), F32)],
        compiler_params=PARAMS,
        name="place",
    )(sub.reshape(1), arrived)

    n_dev = n_dom * n_sub
    both = ("dom", "sub")
    peer = lax.ppermute(for_peer, both, [(i, i ^ 1) for i in range(n_dev)])
    edge = pl.pallas_call(
        edge_kernel,
        out_shape=jax.ShapeDtypeStruct((halo, flat), BF16),
        in_specs=[smem, vmem, vmem],
        out_specs=vmem,
        compiler_params=PARAMS,
        name="edge",
    )(sub.reshape(1), mine, peer)
    across = [pair for i in range(1, n_dev - 1, 2) for pair in ((i, i + 1), (i + 1, i))]
    edge = lax.ppermute(edge, both, across)

    base = device * rows_dev - sub * halo
    rows = modes * neigh
    inner = rows_dev - halo
    chunk = 8
    out_shape = jax.ShapeDtypeStruct((rows_dev, rows, width), F32)
    left_shape = VMEM((rows_dev * rows, width), F32)
    begun, rest = pl.pallas_call(
        inner_kernel,
        out_shape=[out_shape, jax.ShapeDtypeStruct((halo, neigh * width, width), BF16)],
        in_specs=[smem, smem] + [vmem] * 4 + [hbm],
        out_specs=[hbm, vmem],
        scratch_shapes=[
            left_shape,
            VMEM((inner, neigh * width, width), BF16),
            VMEM((inner, rows, width), F32),
            pltpu.SemaphoreType.DMA((inner // chunk + 1,)),
            pltpu.SemaphoreType.DMA((inner // chunk,)),
        ],
        compiler_params=pltpu.CompilerParams(vmem_limit_bytes=48 * MIB),
        cost_estimate=pl.CostEstimate(
            flops=2 * inner * rows * neigh * width * width, bytes_accessed=tiles_a.size * 2, transcendentals=0
        ),
        name="inner",
    )(sub.reshape(1), base.reshape(1), tile_cols.T, mine, peer, inv_diag, turned)
    out = pl.pallas_call(
        outer_kernel,
        out_shape=out_shape,
        in_specs=[smem, smem] + [vmem] * 6 + [hbm],
        out_specs=hbm,
        scratch_shapes=[left_shape, VMEM((halo, rows, width), F32), pltpu.SemaphoreType.DMA],
        input_output_aliases={8: 0},
        compiler_params=PARAMS,
        name="outer",
    )(sub.reshape(1), base.reshape(1), tile_cols.T, mine, peer, edge, inv_diag, rest, begun)
    return jnp.transpose(out.reshape(rows_dev, modes, neigh, width), (0, 2, 1, 3))


def solution(mesh):
    in_specs = (
        P(("dom", "sub"), None, None),
        P(("dom", "sub")),
        P(("dom", "sub")),
        P(("dom", "sub"), None, None, None),
        P(("dom", "sub"), None),
        P(("dom", "sub"), None),
    )
    out_specs = P(("dom", "sub"), None, None, None)
    return jax.shard_map(
        per_device, mesh=mesh, in_specs=in_specs, out_specs=out_specs, check_vma=False
    )
```

```python
import jax
import jax.numpy as jnp
from jax import lax
from jax.experimental import pallas as pl
from jax.experimental.pallas import tpu as pltpu
from jax.sharding import PartitionSpec as P

DAMPING = 2.0 / 3.0
BF16 = jnp.bfloat16
F32 = jnp.float32
VMEM = pltpu.VMEM
SMEM = pltpu.SMEM

LANES = 128
MIB = 2**20
PARAMS = pltpu.CompilerParams(vmem_limit_bytes=20 * MIB)
MIDDLE = pltpu.CompilerParams(vmem_limit_bytes=48 * MIB)
WIDE = pltpu.CompilerParams(vmem_limit_bytes=60 * MIB)
PARTS = ((0, 24), (24, 48))
MSG_ROWS = 14


def partition_of(message):
    z, x, y = message % 8, message // 8 % 4, message // 32
    return 127 - (z * 16 + y * 4 + x)


ORDER = [partition_of(i) for i in range(128)]


def iota(shape, dim):
    return lax.broadcasted_iota(jnp.int32, shape, dim)


def dot(a, b, dims):
    return lax.dot_general(a, b, (dims, ((), ())), preferred_element_type=F32)


def onehot(cond):
    return jnp.where(cond, 1.0, 0.0).astype(BF16)


def pack_kernel(count_hbm, agg_hbm, pt_hbm, out_ref, wide, count_ref, agg_ref, pt_ref, sems):
    modes, slots, _ = pt_ref.shape
    n_dom = out_ref.shape[0] // MSG_ROWS
    copies = [
        pltpu.make_async_copy(count_hbm, count_ref, sems.at[0]),
        pltpu.make_async_copy(agg_hbm, agg_ref, sems.at[1]),
        pltpu.make_async_copy(pt_hbm, pt_ref, sems.at[2]),
    ]
    for copy in copies:
        copy.start()
    copies[0].wait()
    copies[1].wait()
    agg = agg_ref[...]
    live = iota((1, slots), 1) < count_ref[0]
    owner = jnp.where(live, agg // LANES, -1)
    position = agg % LANES
    to_dest = owner == partition_of(iota((n_dom, slots), 0))
    before = onehot(iota((slots, slots), 0) < iota((slots, slots), 1))
    rank = dot(onehot(to_dest), before, ((1,), (0,)))
    first = onehot(to_dest & (rank < 0.5))
    second = onehot(to_dest & (rank > 0.5))
    pick = jnp.concatenate([first, second], axis=0)
    at = onehot(position == iota((LANES, slots), 0))
    where_to = dot(pick, at, ((1,), (1,)))
    copies[2].wait()
    blocks = jnp.concatenate([pt_ref[c].astype(BF16) for c in range(modes)], axis=1)
    sent = dot(pick, blocks, ((1,), (0,)))
    for r in range(2):
        rows = slice(r * n_dom, (r + 1) * n_dom)
        for c in range(modes):
            wide[pl.ds(r * modes + c, n_dom, stride=MSG_ROWS), :] = sent[rows, c * LANES : (c + 1) * LANES]
        wide[pl.ds(2 * modes + r, n_dom, stride=MSG_ROWS), :] = where_to[rows]
    out_ref[...] = wide[...].astype(BF16)


def place_kernel(sub_ref, msg_ref, mine_ref, peer_ref, wide, placed):
    n_dom = msg_ref.shape[0] // MSG_ROWS
    modes = MSG_ROWS // 2 - 1
    keep = mine_ref.shape[0]
    sub = sub_ref[0]
    wide[...] = msg_ref[...].astype(F32)

    def column(row):
        return wide[pl.ds(row, n_dom, stride=MSG_ROWS), :].astype(BF16)

    at = jnp.concatenate([column(2 * modes + r) for r in range(2)], axis=0)
    blocks = jnp.concatenate(
        [jnp.concatenate([column(r * modes + c) for c in range(modes)], axis=1) for r in range(2)], axis=0
    )
    placed[...] = dot(at, blocks, ((0,), (0,)))
    low = pl.multiple_of(sub * (LANES - keep), 16)
    mine_ref[...] = placed[pl.ds(low, keep), :].astype(BF16)
    other = pl.multiple_of((1 - sub) * (LANES - keep), 16)
    peer_ref[...] = placed[pl.ds(other, keep), :].astype(BF16)


def edge_kernel(sub_ref, mine_ref, peer_ref, edge_ref):
    keep, halo = mine_ref.shape[0], edge_ref.shape[0]
    low = pl.multiple_of(sub_ref[0] * (keep - halo), 16)
    edge_ref[...] = mine_ref[pl.ds(low, halo), :] + peer_ref[pl.ds(low, halo), :]


def turn_kernel(sub_ref, tiles_ref, out_ref, rest_ref):
    step = pl.program_id(0)
    n_tile, neigh, width, _ = tiles_ref.shape
    for n in range(n_tile):
        for k in range(neigh):
            out_ref[n, k * width : (k + 1) * width, :] = tiles_ref[n, k].T

    @pl.when(step == sub_ref[0] * (pl.num_programs(0) - 1))
    def _():
        rest_ref[...] = out_ref[...]


def gather(ext, local, left, neigh, modes):
    total = local.shape[1]
    for k in range(neigh):
        take = onehot(iota((ext.shape[0], total), 0) == local[k : k + 1, :])
        got = dot(take, ext, ((0,), (0,)))
        for c in range(modes):
            left[pl.ds(c * neigh + k, total, stride=modes * neigh), :] = got[:, c * LANES : (c + 1) * LANES]


def smooth_row(n, t, left, tiles, diag_ref, neigh, rows):
    lhs = left[n * rows : (n + 1) * rows, :]
    row_k = iota((rows, LANES), 0) % neigh
    spread = jnp.concatenate([jnp.where(row_k == k, lhs, 0.0).astype(BF16) for k in range(neigh)], axis=1)
    product = dot(spread, tiles, ((1,), (0,)))
    scale = -DAMPING * diag_ref[pl.ds(t, 1), :]
    return scale * product + jnp.where(row_k == 0, lhs, 0.0)


def inner_kernel(
    sub_ref, base_ref, cols_ref, mine_ref, peer_ref, diag_ref, tiles_hbm, done_ref, left, tiles, sems
):
    count, rows, _ = done_ref.shape
    neigh = cols_ref.shape[0]
    start = (1 - sub_ref[0]) * (tiles_hbm.shape[0] - count)
    fetches = []
    for i, (low, high) in enumerate(PARTS):
        there, here = pl.ds(start + low, high - low), pl.ds(low, high - low)
        fetches.append(pltpu.make_async_copy(tiles_hbm.at[there], tiles.at[here], sems.at[i]))
        fetches[-1].start()
    gather(mine_ref[...] + peer_ref[...], cols_ref[...] - base_ref[0], left, neigh, rows // neigh)
    for fetch, (low, high) in zip(fetches, PARTS):
        fetch.wait()
        for n in range(low, high):
            done_ref[n] = smooth_row(n, start + n, left, tiles[n], diag_ref, neigh, rows)


def outer_kernel(
    sub_ref, base_ref, cols_ref, mine_ref, peer_ref, edge_ref, diag_ref, rest_ref, inner_ref, out_hbm, left, done, sems
):
    count, rest = inner_ref.shape[0], done.shape[0]
    rows, neigh = done.shape[1], cols_ref.shape[0]
    write_inner = pltpu.make_async_copy(inner_ref, out_hbm.at[pl.ds((1 - sub_ref[0]) * rest, count)], sems.at[0])
    write_inner.start()
    start = sub_ref[0] * count
    ext = jnp.concatenate([mine_ref[...] + peer_ref[...], edge_ref[...]], axis=0)
    local = cols_ref[...] - base_ref[0]
    gather(ext, jnp.where(local < 0, local + ext.shape[0], local), left, neigh, rows // neigh)
    for n in range(rest):
        done[n] = smooth_row(n, start + n, left, rest_ref[n], diag_ref, neigh, rows)
    write = pltpu.make_async_copy(done, out_hbm.at[pl.ds(start, rest)], sems.at[1])
    write.start()
    write_inner.wait()
    write.wait()


def per_device(pt_old, agg_index, counts, tiles_a, tile_cols, inv_diag):
    n_dom = lax.axis_size("dom")
    n_sub = lax.axis_size("sub")
    slots, modes, width = pt_old.shape
    rows_dev, neigh = tile_cols.shape
    halo = rows_dev // 4
    keep = rows_dev + halo
    sub = lax.axis_index("sub")
    device = lax.axis_index("dom") * n_sub + sub
    vmem = pl.BlockSpec(memory_space=VMEM)
    smem = pl.BlockSpec(memory_space=SMEM)

    hbm = pl.BlockSpec(memory_space=pl.ANY)
    flat = modes * width
    msg_shape = (n_dom * MSG_ROWS, width)
    messages = pl.pallas_call(
        pack_kernel,
        out_shape=jax.ShapeDtypeStruct(msg_shape, BF16),
        in_specs=[hbm, hbm, hbm],
        out_specs=vmem,
        scratch_shapes=[
            VMEM(msg_shape, F32),
            SMEM((1,), jnp.int32),
            VMEM((1, slots), jnp.int32),
            VMEM((modes, slots, width), F32),
            pltpu.SemaphoreType.DMA((3,)),
        ],
        compiler_params=WIDE,
        name="pack",
    )(counts, agg_index.reshape(1, slots), jnp.transpose(pt_old, (1, 0, 2)))

    messages, tiles_a = lax.optimization_barrier((messages, tiles_a))
    arrived = lax.all_to_all(
        messages.reshape(n_dom, MSG_ROWS // 2, 2, width),
        "dom",
        split_axis=0,
        concat_axis=0,
        tiled=True,
        axis_index_groups=[ORDER],
    ).reshape(msg_shape)

    turned, rest = pl.pallas_call(
        turn_kernel,
        out_shape=[jax.ShapeDtypeStruct((n, neigh * width, width), BF16) for n in (rows_dev, halo)],
        grid=(rows_dev // halo,),
        in_specs=[smem, pl.BlockSpec((halo, neigh, width, width), lambda i: (i, 0, 0, 0))],
        out_specs=[
            pl.BlockSpec((halo, neigh * width, width), lambda i: (i, 0, 0)),
            pl.BlockSpec((halo, neigh * width, width), lambda i: (0, 0, 0)),
        ],
        compiler_params=WIDE,
        cost_estimate=pl.CostEstimate(flops=0, bytes_accessed=2 * tiles_a.size * 2, transcendentals=0),
        name="turn",
    )(sub.reshape(1), tiles_a)
    inner = rows_dev - halo
    inner_cols = lax.dynamic_slice_in_dim(tile_cols, (1 - sub) * halo, inner, 0).T
    outer_cols = lax.dynamic_slice_in_dim(tile_cols, sub * inner, halo, 0).T
    arrived, turned, rest, inner_cols, outer_cols = lax.optimization_barrier(
        (arrived, turned, rest, inner_cols, outer_cols)
    )

    mine, for_peer = pl.pallas_call(
        place_kernel,
        out_shape=[jax.ShapeDtypeStruct((keep, flat), BF16)] * 2,
        in_specs=[smem, vmem],
        out_specs=[vmem] * 2,
        scratch_shapes=[VMEM(msg_shape, F32), VMEM((LANES, flat), F32)],
        compiler_params=PARAMS,
        name="place",
    )(sub.reshape(1), arrived)

    n_dev = n_dom * n_sub
    both = ("dom", "sub")
    peer = lax.ppermute(for_peer, both, [(i, i ^ 1) for i in range(n_dev)])
    edge = pl.pallas_call(
        edge_kernel,
        out_shape=jax.ShapeDtypeStruct((halo, flat), BF16),
        in_specs=[smem, vmem, vmem],
        out_specs=vmem,
        compiler_params=PARAMS,
        name="edge",
    )(sub.reshape(1), mine, peer)
    across = [pair for i in range(1, n_dev - 1, 2) for pair in ((i, i + 1), (i + 1, i))]
    edge = lax.ppermute(edge, both, across)

    base = device * rows_dev - sub * halo
    rows = modes * neigh
    inner_out = pl.pallas_call(
        inner_kernel,
        out_shape=jax.ShapeDtypeStruct((inner, rows, width), F32),
        in_specs=[smem, smem] + [vmem] * 4 + [hbm],
        out_specs=vmem,
        scratch_shapes=[
            VMEM((inner * rows, width), F32),
            VMEM((inner, neigh * width, width), BF16),
            pltpu.SemaphoreType.DMA((len(PARTS),)),
        ],
        compiler_params=MIDDLE,
        cost_estimate=pl.CostEstimate(
            flops=2 * inner * rows * neigh * width * width, bytes_accessed=tiles_a.size * 2, transcendentals=0
        ),
        name="inner",
    )(sub.reshape(1), base.reshape(1), inner_cols, mine, peer, inv_diag, turned)
    out = pl.pallas_call(
        outer_kernel,
        out_shape=jax.ShapeDtypeStruct((rows_dev, rows, width), F32),
        in_specs=[smem, smem] + [vmem] * 7,
        out_specs=hbm,
        scratch_shapes=[
            VMEM((halo * rows, width), F32),
            VMEM((halo, rows, width), F32),
            pltpu.SemaphoreType.DMA((2,)),
        ],
        compiler_params=PARAMS,
        name="outer",
    )(sub.reshape(1), base.reshape(1), outer_cols, mine, peer, edge, inv_diag, rest, inner_out)
    return jnp.transpose(out.reshape(rows_dev, modes, neigh, width), (0, 2, 1, 3))


def solution(mesh):
    in_specs = (
        P(("dom", "sub"), None, None),
        P(("dom", "sub")),
        P(("dom", "sub")),
        P(("dom", "sub"), None, None, None),
        P(("dom", "sub"), None),
        P(("dom", "sub"), None),
    )
    out_specs = P(("dom", "sub"), None, None, None)
    return jax.shard_map(
        per_device, mesh=mesh, in_specs=in_specs, out_specs=out_specs, check_vma=False
    )
```
